1024 devices in a mesh: tile: 128 (over x, z_hi, y, core), bin: 8 (over z_lo).
Axes of the slice: x: 4, y: 4, z: 32 (z_hi: 4, z_lo: 8; z = z_hi * 8 + z_lo), core: 2. Of those that a mesh axis runs over, the one named last changes fastest.
Arguments:
- dust_density: float32 [128, 1024, 512], P('bin', 'tile'), may hold values from 0.05 to 2
- dust_vr: float32 [128, 1024, 512], P('bin', 'tile'), may hold values from -1 to 1
- dust_va: float32 [128, 1024, 512], P('bin', 'tile'), may hold values from -1 to 1
- gas_density: float32 [1024, 512], P('tile'), may hold values from 0.5 to 2
- gas_vr: float32 [1024, 512], P('tile'), may hold values from -1 to 1
- gas_va: float32 [1024, 512], P('tile'), may hold values from -1 to 1
- stop_time: float32 [128], P('bin'), may hold values from 0.05 to 20
- gain_coef: bfloat16 [128, 128, 128], P('bin'), may hold values from -0.046875 to 0.046875
Outputs:
- density_out: float32 [128, 1024, 512], P('bin', 'tile')
- vr_out: float32 [128, 1024, 512], P('bin', 'tile')
- va_out: float32 [128, 1024, 512], P('bin', 'tile')
- gas_vr_out: float32 [1024, 512], P('tile')
- gas_va_out: float32 [1024, 512], P('tile')
The draws below stay inside these ranges and needn't reach their ends.
All inputs are finite; a program needn't handle non-finite values.
Results may differ from the reference program's by a relative error of at most 0.0017.
Values may be sent and summed in bfloat16 or wider, within the bound.
A program may use at most 32 MiB of HBM per device.

```python
import math
import jax
import jax.numpy as jnp
from jax import lax

NA = 512
BINS = 128
NR = 1024


def steps_of(own_key, shape, cuts, low, high):
    def one(position, blocks):
        steps = jax.random.uniform(jax.random.fold_in(jax.random.fold_in(own_key, 6), position), (blocks,), jnp.float32, low / len(cuts), high / len(cuts))
        return jnp.repeat(jnp.exp(steps), shape[position] // blocks).reshape((-1,) + (1,) * (len(shape) - position - 1))

    factor_of = one(*cuts[0])
    for cut in cuts[1:]:
        factor_of = factor_of * one(*cut)
    return factor_of


def normal_values(key, extent, spread, reach, pieces=(), dtype=jnp.bfloat16):
    values = jax.random.normal(key, extent, jnp.float32) * spread
    if len(pieces) > 0:
        values = steps_of(key, extent, pieces, -0.22, 0.18) * values
    return jnp.clip(values, min=-reach, max=reach).astype(dtype)


def setup_inputs(seed: int = 0) -> dict:
    keys = jax.random.split(jax.random.key(seed), 9)
    return {
        "dust_density": jnp.clip(jnp.exp(math.log(2.0) - 3.6888794 * jax.random.uniform(keys[0], (BINS, NR, NA), jnp.float32) ** steps_of(keys[0], (BINS, NR, NA), ((0, 8), (1, 128)), -0.2, 0.2)), 0.05, 2.0),
        "dust_vr": jnp.clip(jax.random.uniform(keys[1], (BINS, NR, NA), jnp.float32, -1.0, 1.0) * steps_of(keys[1], (BINS, NR, NA), ((0, 8), (1, 128)), -0.4, 0.0), -1.0, 1.0),
        "dust_va": jnp.clip(jax.random.uniform(keys[2], (BINS, NR, NA), jnp.float32, -1.0, 1.0) * steps_of(keys[2], (BINS, NR, NA), ((0, 8), (1, 128)), -0.4, 0.0), -1.0, 1.0),
        "gas_density": jnp.clip(0.5 + 1.5 * jax.random.uniform(keys[3], (NR, NA), jnp.float32) ** steps_of(keys[3], (NR, NA), ((0, 128),), -0.2, 0.2), 0.5, 2.0),
        "gas_vr": jnp.clip(jax.random.uniform(keys[4], (NR, NA), jnp.float32, -1.0, 1.0) * steps_of(keys[4], (NR, NA), ((0, 128),), -0.4, 0.0), -1.0, 1.0),
        "gas_va": jnp.clip(jax.random.uniform(keys[5], (NR, NA), jnp.float32, -1.0, 1.0) * steps_of(keys[5], (NR, NA), ((0, 128),), -0.4, 0.0), -1.0, 1.0),
        "stop_time": jnp.clip(jnp.exp(math.log(20.0) - 5.9914645 * jax.random.uniform(keys[6], (BINS,), jnp.float32) ** steps_of(keys[6], (BINS,), ((0, 8),), -0.2, 0.2)), 0.05, 20.0),
        "gain_coef": normal_values(keys[7], (BINS, BINS, BINS), (BINS * BINS) ** -0.5, 0.046875, ((0, 8),)),
    }


COURANT = 0.2
COAGULATION = 0.5


def minmod(first, second):
    smaller = jnp.sign(first) * jnp.minimum(jnp.abs(first), jnp.abs(second))
    return jnp.where(first * second > 0, smaller, jnp.zeros_like(first))


def faces_div(values, speeds, along):
    length = values.shape[along]

    def part(array, lower, upper_cut):
        return lax.slice_in_dim(array, lower, length - upper_cut, axis=along)

    slope = minmod(part(values, 1, 1) - part(values, 0, 2), part(values, 2, 0) - part(values, 1, 1))
    centre = part(values, 1, 1)
    centre_speed = part(speeds, 1, 1)
    inner_len = length - 2

    def sub(array, lower, upper_cut):
        return lax.slice_in_dim(array, lower, inner_len - upper_cut, axis=along)

    speed = 0.5 * (sub(centre_speed, 0, 1) + sub(centre_speed, 1, 0))
    left = sub(centre, 0, 1) + 0.5 * (1.0 - speed * COURANT) * sub(slope, 0, 1)
    right = sub(centre, 1, 0) - 0.5 * (1.0 + speed * COURANT) * sub(slope, 1, 0)
    flux = jnp.maximum(speed, 0.0) * left + jnp.minimum(speed, 0.0) * right
    face_count = inner_len - 1
    return lax.slice_in_dim(flux, 1, face_count, axis=along) - lax.slice_in_dim(flux, 0, face_count - 1, axis=along)


def wrap_azimuth(field):
    return jnp.concatenate([field[..., -2:], field, field[..., :2]], axis=-1)


def reference(dust_density, dust_vr, dust_va, gas_density, gas_vr, gas_va, stop_time, gain_coef):
    padded_rho = jnp.pad(dust_density, ((0, 0), (2, 2), (0, 0)))
    padded_speed = jnp.pad(dust_vr, ((0, 0), (2, 2), (0, 0)))
    radial_div = faces_div(padded_rho, padded_speed, 1)
    azimuth_div = faces_div(wrap_azimuth(dust_density), wrap_azimuth(dust_va), 2)
    density_adv = dust_density - COURANT * (radial_div + azimuth_div)
    drag_rate = 1.0 / stop_time
    coupling = drag_rate / (1.0 + drag_rate)
    weight = density_adv * coupling[:, None, None]
    sum_radial = jnp.sum(weight * dust_vr, axis=0)
    sum_azimuth = jnp.sum(weight * dust_va, axis=0)
    sum_weight = jnp.sum(weight, axis=0)
    denom = gas_density + sum_weight
    gas_vr_out = (gas_density * gas_vr + sum_radial) / denom
    gas_va_out = (gas_density * gas_va + sum_azimuth) / denom
    rate_col = drag_rate[:, None, None]
    vr_out = (dust_vr + rate_col * gas_vr_out[None]) / (1.0 + rate_col)
    va_out = (dust_va + rate_col * gas_va_out[None]) / (1.0 + rate_col)
    bin_total = dust_density.shape[0]
    density_low = density_adv.astype(jnp.bfloat16).reshape(bin_total, -1)
    density_wide = density_low.astype(jnp.float32)

    def one_bin(coef_slice):
        inner = jnp.dot(coef_slice, density_low, preferred_element_type=jnp.float32)
        return jnp.sum(density_wide * inner, axis=0)

    gain = lax.map(one_bin, gain_coef).reshape(density_adv.shape)
    density_out = density_adv + COAGULATION * gain
    return density_out, vr_out, va_out, gas_vr_out, gas_va_out
```

```python
import functools

import jax
import jax.numpy as jnp
from jax import lax
from jax.experimental import pallas as pl
from jax.experimental.pallas import tpu as pltpu
from jax.sharding import PartitionSpec as P

COURANT = 0.2
COAGULATION = 0.5
TILE_SPLIT = {128: (4, 4, 4, 2)}
QUAD = 4
ROWS = 8
LANES = 128
CHUNKS = 4
VMEM_BYTES = 40 * 2**20
ROW_ORDER = (2, 3, 4, 5, 0, 1, 6, 7)
MESH = pl.DeviceIdType.MESH
F32 = jnp.float32
BF16 = jnp.bfloat16


def minmod(a, b):
    return jnp.maximum(jnp.minimum(a, b), 0.0) + jnp.minimum(jnp.maximum(a, b), 0.0)


def face_flux(q, q_next, s, s_next, v, v_next):
    u = 0.5 * (v + v_next)
    forward = u > 0
    reach = 0.5 - 0.5 * COURANT * jnp.abs(u)
    return u * (jnp.where(forward, q, q_next) + reach * jnp.where(forward, s, -s_next))


def azimuth_div(q, v):
    cells = q.shape[1]

    def ahead(x):
        return pltpu.roll(x, cells - 1, 1)

    def behind(x):
        return pltpu.roll(x, 1, 1)

    q_next = ahead(q)
    step = q_next - q
    s = minmod(behind(step), step)
    flux = face_flux(q, q_next, s, ahead(s), v, ahead(v))
    return flux - behind(flux)


def kernel(
    split,
    tiles,
    rho_hbm,
    vr_hbm,
    va_hbm,
    coef_hbm,
    stop,
    gas_rho_hbm,
    gas_vr_hbm,
    gas_va_hbm,
    tiles_out,
    gas_out,
    tiles_in,
    gas_in,
    own_coef,
    mate_coef,
    q_rows,
    v_rows,
    a_rows,
    edge_send,
    edge_recv,
    adv,
    halves,
    all_bins,
    partial,
    partial_in,
    quad_sum,
    gas_rows,
    gain_send,
    gain_recv,
    load_sem,
    halo_send,
    halo_recv,
    give_send,
    item_recv,
    up_send,
    down_send,
    gain_send_sem,
    gain_recv_sem,
    coef_send,
    coef_recv,
    sum_send,
    sum_recv,
):
    xs, hs, ys, cores = split
    bins, cells = q_rows.shape[1:]
    half = cells // 2
    lane_tiles = cells // LANES
    t = lax.axis_index("tile")
    z = lax.axis_index("bin")
    core = t % cores
    y = (t // cores) % ys
    z_hi = (t // (cores * ys)) % hs
    x = t // (cores * ys * hs)
    w = z % QUAD
    quad = z // QUAD
    mate = (z + QUAD) % (2 * QUAD)
    own_base = quad * QUAD
    other_base = QUAD - own_base

    def tile_at(x_, y_, core_):
        return ((x_ * hs + z_hi) * ys + y_) * cores + core_

    def quad_at(i):
        return own_base + (w + i) % QUAD

    def lane_tile(l):
        return pl.ds(l * LANES, LANES)

    loads = [
        [
            pltpu.make_async_copy(src.at[:, lane_tile(l)], tiles_in.at[i, l], load_sem.at[i, l])
            for l in range(lane_tiles)
        ]
        for i, src in enumerate((rho_hbm, vr_hbm, va_hbm))
    ]
    load_coef = pltpu.make_async_copy(coef_hbm, own_coef, load_sem.at[3, 0])
    load_gas = [
        pltpu.make_async_copy(src, gas_in.at[i], load_sem.at[3, 1 + i])
        for i, src in enumerate((gas_rho_hbm, gas_vr_hbm, gas_va_hbm))
    ]
    for group in loads:
        for load in group:
            load.start()
    load_coef.start()
    for load in load_gas:
        load.start()

    barrier = pltpu.get_barrier_semaphore()
    peers = [(t, mate)] + [(t, quad_at(i)) for i in range(1, QUAD)]
    peers += [(tile_at(x, (y + i) % ys, core), z) for i in range(1, ys)]
    peers += [(tile_at((x + i) % xs, y, core), z) for i in range(1, xs)]
    peers += [((t + 1) % tiles, z), ((t + tiles - 1) % tiles, z)]
    for peer in peers:
        pl.semaphore_signal(barrier, inc=1, device_id=peer, device_id_type=MESH)

    has_prev = t > 0
    has_next = t < tiles - 1
    prev_dev = (jnp.maximum(t - 1, 0), z)
    next_dev = (jnp.minimum(t + 1, tiles - 1), z)

    stop_bin = lax.broadcasted_iota(jnp.int32, (bins, 1), 0)
    stop_col = jnp.zeros((bins, 1), F32)
    for b in range(bins):
        stop_col = jnp.where(stop_bin == b, stop[b], stop_col)
    couple = 1.0 / (1.0 + stop_col)
    keep = stop_col * couple

    partial[...] = jnp.zeros_like(partial)
    for group, rows, first in zip(loads, (q_rows, v_rows, a_rows), (2, 1, 0)):
        i = 2 - first
        for l, load in enumerate(group):
            load.wait()
            for r in range(ROWS):
                rows[first + r, :, lane_tile(l)] = tiles_in[i, l, pl.ds(r, bins, stride=ROWS), :]

    def put(i, r, value):
        for l in range(lane_tiles):
            tiles_out[i, l, pl.ds(r, bins, stride=ROWS), :] = value[:, l * LANES : (l + 1) * LANES]

    for i, (first, speed) in enumerate(((ROWS, ROWS), (2, 1))):
        edge_send[i, 0:2] = q_rows[first : first + 2].astype(BF16)
        edge_send[i, 2] = v_rows[speed].astype(BF16)

    pl.semaphore_wait(barrier, len(peers))

    def halo(i, device):
        return pltpu.make_async_remote_copy(
            src_ref=edge_send.at[i],
            dst_ref=edge_recv.at[i],
            send_sem=halo_send.at[i],
            recv_sem=halo_recv.at[i],
            device_id=device,
            device_id_type=MESH,
        )

    to_next, to_prev = halo(0, next_dev), halo(1, prev_dev)

    @pl.when(has_next)
    def _():
        to_next.start()

    @pl.when(has_prev)
    def _():
        to_prev.start()

    piece_rows = mate_coef.shape[3]
    piece = (core * xs + x) * ys + y

    def coef_copy(i, src, dst, device):
        return pltpu.make_async_remote_copy(
            src_ref=src,
            dst_ref=dst,
            send_sem=coef_send.at[i],
            recv_sem=coef_recv.at[i],
            device_id=device,
            device_id_type=MESH,
        )

    coef_from_mate = coef_copy(
        0,
        coef_hbm.at[pl.ds(pl.multiple_of(piece * piece_rows, piece_rows), piece_rows)],
        mate_coef.at[core, x, y],
        (t, mate),
    )
    coef_y = [
        coef_copy(i, mate_coef.at[core, x, y], mate_coef.at[core, x, y], (tile_at(x, (y + i) % ys, core), z))
        for i in range(1, ys)
    ]
    coef_x = [
        coef_copy(3 + i, mate_coef.at[core, x], mate_coef.at[core, x], (tile_at((x + i) % xs, y, core), z))
        for i in range(1, xs)
    ]
    coef_core = [
        coef_copy(6 + i, mate_coef.at[core], mate_coef.at[core], (tile_at(x, y, (core + i) % cores), z))
        for i in range(1, cores)
    ]

    def give(c):
        return pltpu.make_async_remote_copy(
            src_ref=halves.at[c, 1 - quad],
            dst_ref=all_bins.at[c, z],
            send_sem=give_send.at[c],
            recv_sem=item_recv.at[c, z],
            device_id=(t, mate),
            device_id_type=MESH,
        )

    def taken(c):
        return pltpu.make_async_remote_copy(
            src_ref=halves.at[c, 1 - quad],
            dst_ref=all_bins.at[c, mate],
            send_sem=give_send.at[c],
            recv_sem=item_recv.at[c, mate],
            device_id=(t, mate),
            device_id_type=MESH,
        )

    def pass_on(c, d, place, up):
        return pltpu.make_async_remote_copy(
            src_ref=all_bins.at[c, d],
            dst_ref=all_bins.at[c, d],
            send_sem=(up_send if up else down_send).at[place],
            recv_sem=item_recv.at[c, d],
            device_id=(t, jnp.minimum(z + 1, 2 * QUAD - 1) if up else jnp.maximum(z - 1, 0)),
            device_id_type=MESH,
        )

    can_up = w < QUAD - 1
    can_down = w > 0

    def send_both(c, d):
        @pl.when(can_up)
        def _():
            pass_on(c, d, w, True).start()

        @pl.when(can_down)
        def _():
            pass_on(c, d, w, False).start()

    def relay(c, far):
        @pl.when(w >= far)
        def _():
            for base in (own_base, other_base):
                d = base + jnp.maximum(w - far, 0)
                pass_on(c, d, jnp.maximum(w - far, 0), True).wait_recv()
                if far < QUAD - 1:

                    @pl.when(can_up)
                    def _():
                        pass_on(c, d, jnp.maximum(w - far, 0), True).start()

        @pl.when(w + far < QUAD)
        def _():
            for base in (own_base, other_base):
                d = base + jnp.minimum(w + far, QUAD - 1)
                pass_on(c, d, jnp.minimum(w + far, QUAD - 1), False).wait_recv()
                if far < QUAD - 1:

                    @pl.when(can_down)
                    def _():
                        pass_on(c, d, jnp.minimum(w + far, QUAD - 1), False).start()

    def take_mates(c):
        taken(c).wait_recv()
        send_both(c, mate)

    def slope(i):
        return minmod(q_rows[i] - q_rows[i - 1], q_rows[i + 1] - q_rows[i])

    def radial_flux(r):
        return face_flux(
            q_rows[r + 1], q_rows[r + 2], slope(r + 1), slope(r + 2), v_rows[r], v_rows[r + 1]
        )

    def advect(c):
        before = None
        for j in range(2):
            r = ROW_ORDER[2 * c + j]
            if before is None:
                before = radial_flux(r)
            after = radial_flux(r + 1)
            v_a = a_rows[r]
            q = q_rows[2 + r]
            new = q - COURANT * ((after - before) + azimuth_div(q, v_a))
            before = after
            adv[r] = new
            low = new.astype(BF16)
            halves[c, 0, j] = low[:, :half]
            halves[c, 1, j] = low[:, half:]
            weight = new * couple
            for n, term in enumerate((weight * v_rows[1 + r], weight * v_a, weight)):
                partial[r // 2, pl.ds(3 * j + n, 1), :] = jnp.sum(term, axis=0, keepdims=True)

    def launch(c):
        all_bins[c, z] = halves[c, quad]
        give(c).start()
        send_both(c, z)

    def gains(c, coef, j):
        low = all_bins[c, :, j].reshape(2 * QUAD * bins, half)
        wide = low.astype(F32).reshape(1, 2 * QUAD * bins // 8, 8, half)
        inner = jnp.dot(coef, low, preferred_element_type=F32)
        terms = inner.reshape(bins, 2 * QUAD * bins // 8, 8, half) * wide
        return jnp.sum(jnp.sum(terms, axis=1), axis=1)

    def gain_copy(c):
        return pltpu.make_async_remote_copy(
            src_ref=gain_send.at[c],
            dst_ref=gain_recv.at[c],
            send_sem=gain_send_sem.at[c],
            recv_sem=gain_recv_sem.at[c],
            device_id=(t, mate),
            device_id_type=MESH,
        )

    def mate_gains(c):
        coef = mate_coef[...].reshape(own_coef.shape)
        for j in range(2):
            gain_send[c, j] = gains(c, coef, j).astype(BF16)
        gain_copy(c).start()

    def own_gains(c):
        coef = own_coef[...]
        for j in range(2):
            r = ROW_ORDER[2 * c + j]
            lanes = pl.ds(pl.multiple_of(quad * half, half), half)
            adv[r, :, lanes] = adv[r, :, lanes] + COAGULATION * gains(c, coef, j)

    def finish(c):
        gain_copy(c).wait_recv()
        for j in range(2):
            r = ROW_ORDER[2 * c + j]
            lanes = pl.ds(pl.multiple_of((1 - quad) * half, half), half)
            adv[r, :, lanes] = adv[r, :, lanes] + COAGULATION * gain_recv[c, j].astype(F32)
            put(0, r, adv[r])

    def sum_copy(i, src, dst, device):
        return pltpu.make_async_remote_copy(
            src_ref=src,
            dst_ref=dst,
            send_sem=sum_send.at[i],
            recv_sem=sum_recv.at[i],
            device_id=device,
            device_id_type=MESH,
        )

    spread = [
        sum_copy(i, partial.at[(w + i) % QUAD], partial_in.at[i], (t, quad_at(i))) for i in range(1, QUAD)
    ]
    across = sum_copy(QUAD, quad_sum.at[0], quad_sum.at[1], (t, mate))
    shared = [
        sum_copy(QUAD + i, gas_rows.at[w], gas_rows.at[w], (t, quad_at(i))) for i in range(1, QUAD)
    ]
    shared_in = [
        sum_copy(QUAD + i, gas_rows.at[(w - i + QUAD) % QUAD], gas_rows.at[(w - i + QUAD) % QUAD], (t, quad_at(i)))
        for i in range(1, QUAD)
    ]

    def sum_across():
        total = partial[w]
        for copy in spread:
            copy.wait_recv()
        for i in range(1, QUAD):
            total = total + partial_in[i]
        quad_sum[0] = total
        across.start()

    def gas_step():
        for load in load_gas:
            load.wait()
        across.wait_recv()
        total = quad_sum[0] + quad_sum[1]
        for j in range(2):
            row = pl.ds(2 * w + j, 1)
            dense = gas_in[0, row, :]
            share = 1.0 / (dense + total[3 * j + 2 : 3 * j + 3])
            gas_rows[w, pl.ds(2 * j, 1), :] = (dense * gas_in[1, row, :] + total[3 * j : 3 * j + 1]) * share
            gas_rows[w, pl.ds(2 * j + 1, 1), :] = (dense * gas_in[2, row, :] + total[3 * j + 1 : 3 * j + 2]) * share
        for copy in shared:
            copy.start()

    def dust_speeds():
        for copy in shared_in:
            copy.wait_recv()
        for r in range(ROWS):
            u, j = r // 2, r % 2
            gas_r = gas_rows[u, pl.ds(2 * j, 1), :]
            gas_a = gas_rows[u, pl.ds(2 * j + 1, 1), :]
            gas_out[0, pl.ds(r, 1), :] = gas_r
            gas_out[1, pl.ds(r, 1), :] = gas_a
            put(1, r, v_rows[1 + r] * keep + gas_r * couple)
            put(2, r, a_rows[r] * keep + gas_a * couple)

    def halo_in():
        @pl.when(has_prev)
        def _():
            to_next.wait_recv()
            q_rows[0:2] = edge_recv[0, 0:2].astype(F32)
            v_rows[0] = edge_recv[0, 2].astype(F32)

        @pl.when(t == 0)
        def _():
            q_rows[0:2] = jnp.zeros_like(q_rows[0:2])
            v_rows[0] = jnp.zeros_like(v_rows[0])

        @pl.when(has_next)
        def _():
            to_prev.wait_recv()
            q_rows[ROWS + 2 : ROWS + 4] = edge_recv[1, 0:2].astype(F32)
            v_rows[ROWS + 1] = edge_recv[1, 2].astype(F32)

        @pl.when(t == tiles - 1)
        def _():
            q_rows[ROWS + 2 : ROWS + 4] = jnp.zeros_like(q_rows[0:2])
            v_rows[ROWS + 1] = jnp.zeros_like(v_rows[0])

    coef_from_mate.start()
    advect(0)
    launch(0)
    advect(1)
    launch(1)
    take_mates(0)
    relay(0, 1)
    take_mates(1)
    coef_from_mate.wait_recv()
    for copy in coef_y:
        copy.start()
    relay(1, 1)
    halo_in()
    advect(2)
    launch(2)
    advect(3)
    launch(3)
    for copy in spread:
        copy.start()
    relay(0, 2)
    for copy in coef_y:
        copy.wait_recv()
    for copy in coef_x:
        copy.start()
    relay(1, 2)
    take_mates(2)
    relay(2, 1)
    take_mates(3)
    relay(3, 1)
    load_coef.wait()
    relay(0, 3)
    own_gains(0)
    relay(2, 2)
    sum_across()
    for copy in coef_x:
        copy.wait_recv()
    for copy in coef_core:
        copy.start()
    relay(3, 2)
    relay(1, 3)
    own_gains(1)
    for copy in coef_core:
        copy.wait_recv()
    mate_gains(0)
    mate_gains(1)
    gas_step()
    relay(2, 3)
    mate_gains(2)
    relay(3, 3)
    mate_gains(3)
    own_gains(2)
    dust_speeds()
    own_gains(3)
    for c in range(CHUNKS):
        finish(c)

    @pl.when(has_next)
    def _():
        to_next.wait_send()

    @pl.when(has_prev)
    def _():
        to_prev.wait_send()

    for copy in [coef_from_mate, across] + coef_y + coef_x + coef_core + spread + shared:
        copy.wait_send()
    for c in range(CHUNKS):
        give(c).wait_send()
        gain_copy(c).wait_send()
    for place in range(QUAD):
        for up in (True, False):

            @pl.when((can_up if up else can_down) & (place <= w if up else place >= w))
            def _():
                pltpu.make_async_remote_copy(
                    src_ref=all_bins.at[:, pl.ds(0, 2)],
                    dst_ref=all_bins.at[:, pl.ds(0, 2)],
                    send_sem=(up_send if up else down_send).at[place],
                    recv_sem=item_recv.at[0, 0],
                    device_id=(t, mate),
                    device_id_type=MESH,
                ).wait_send()


def write_out(tiles, gas, rho_out, vr_out, va_out, gas_vr_out, gas_va_out, sem, gas_sem):
    copies = [pltpu.make_async_copy(gas.at[i], out, gas_sem.at[i]) for i, out in enumerate((gas_vr_out, gas_va_out))]
    for i, out in enumerate((rho_out, vr_out, va_out)):
        for l in range(tiles.shape[1]):
            lanes = pl.ds(l * LANES, LANES)
            copies.append(pltpu.make_async_copy(tiles.at[i, l], out.at[:, lanes], sem.at[i, l]))
    for copy in copies:
        copy.start()
    for copy in copies:
        copy.wait()


def step(split, tiles, rho, vr, va, gas_rho, gas_vr, gas_va, stop, coef):
    bins, rows, cells = rho.shape
    half = cells // 2
    flat = (bins * rows, cells)
    total_bins = coef.shape[1]
    xs, _, ys, cores = split
    coef = coef.reshape(bins * total_bins, total_bins)
    dma = pltpu.SemaphoreType.DMA
    hbm = pl.BlockSpec(memory_space=pltpu.HBM)
    vmem = pl.BlockSpec(memory_space=pltpu.VMEM)
    lane_tiles = cells // LANES
    out_shape = [jax.ShapeDtypeStruct(flat, F32)] * 3 + [jax.ShapeDtypeStruct((rows, cells), F32)] * 2
    results = pl.pallas_call(
        functools.partial(kernel, split, tiles),
        out_shape=[
            jax.ShapeDtypeStruct((3, lane_tiles, flat[0], LANES), F32),
            jax.ShapeDtypeStruct((2, rows, cells), F32),
        ],
        in_specs=[hbm] * 4 + [pl.BlockSpec(memory_space=pltpu.SMEM)] + [hbm] * 3,
        out_specs=[vmem] * 2,
        scratch_shapes=[
            pltpu.VMEM((3, lane_tiles, flat[0], LANES), F32),
            pltpu.VMEM((3, rows, cells), F32),
            pltpu.VMEM(coef.shape, BF16),
            pltpu.VMEM((cores, xs, ys, coef.shape[0] // (cores * xs * ys), total_bins), BF16),
            pltpu.VMEM((rows + 4, bins, cells), F32),
            pltpu.VMEM((rows + 2, bins, cells), F32),
            pltpu.VMEM((rows, bins, cells), F32),
            pltpu.VMEM((2, 3, bins, cells), BF16),
            pltpu.VMEM((2, 3, bins, cells), BF16),
            pltpu.VMEM((rows, bins, cells), F32),
            pltpu.VMEM((CHUNKS, 2, 2, bins, half), BF16),
            pltpu.VMEM((CHUNKS, 2 * QUAD, 2, bins, half), BF16),
            pltpu.VMEM((QUAD, 8, cells), F32),
            pltpu.VMEM((QUAD, 8, cells), F32),
            pltpu.VMEM((2, 8, cells), F32),
            pltpu.VMEM((QUAD, 4, cells), F32),
            pltpu.VMEM((CHUNKS, 2, bins, half), BF16),
            pltpu.VMEM((CHUNKS, 2, bins, half), BF16),
            dma((4, lane_tiles)),
            dma((2,)),
            dma((2,)),
            dma((CHUNKS,)),
            dma((CHUNKS, 2 * QUAD)),
            dma((QUAD,)),
            dma((QUAD,)),
            dma((CHUNKS,)),
            dma((CHUNKS,)),
            dma((8,)),
            dma((8,)),
            dma((2 * QUAD,)),
            dma((2 * QUAD,)),
        ],
        compiler_params=pltpu.CompilerParams(
            collective_id=0, has_side_effects=True, vmem_limit_bytes=VMEM_BYTES
        ),
    )(
        *(pltpu.with_memory_space_constraint(x, pltpu.HBM) for x in (rho.reshape(flat), vr.reshape(flat), va.reshape(flat), coef)),
        stop,
        *(pltpu.with_memory_space_constraint(x, pltpu.HBM) for x in (gas_rho, gas_vr, gas_va)),
    )
    outs = pl.pallas_call(
        write_out,
        out_shape=out_shape,
        in_specs=[vmem] * 2,
        out_specs=[hbm] * 5,
        scratch_shapes=[dma((3, lane_tiles)), dma((2,))],
        compiler_params=pltpu.CompilerParams(vmem_limit_bytes=VMEM_BYTES),
    )(*results)
    return tuple(out.reshape(rho.shape) for out in outs[:3]) + tuple(outs[3:])


def solution(mesh):
    tiles = mesh.shape["tile"]
    grid = P("bin", "tile", None)
    gas = P("tile", None)
    return jax.shard_map(
        functools.partial(step, TILE_SPLIT[tiles], tiles),
        mesh=mesh,
        in_specs=(grid, grid, grid, gas, gas, gas, P("bin"), P("bin", None, None)),
        out_specs=(grid, grid, grid, gas, gas),
        check_vma=False,
    )
```

```python
import functools

import jax
import jax.numpy as jnp
from jax import lax
from jax.experimental import pallas as pl
from jax.experimental.pallas import tpu as pltpu
from jax.sharding import PartitionSpec as P

COURANT = 0.2
COAGULATION = 0.5
TILE_SPLIT = {128: (4, 4, 4, 2)}
QUAD = 4
ROWS = 8
LANES = 128
CHUNKS = 2
DEEP = ROWS // CHUNKS
VMEM_BYTES = 40 * 2**20
ROW_ORDER = (2, 3, 4, 5, 0, 1, 6, 7)
MESH = pl.DeviceIdType.MESH
F32 = jnp.float32
BF16 = jnp.bfloat16


def minmod(a, b):
    return jnp.maximum(jnp.minimum(a, b), 0.0) + jnp.minimum(jnp.maximum(a, b), 0.0)


def face_flux(q, q_next, s, s_next, v, v_next):
    u = 0.5 * (v + v_next)
    forward = u > 0
    reach = 0.5 - 0.5 * COURANT * jnp.abs(u)
    return u * (jnp.where(forward, q, q_next) + reach * jnp.where(forward, s, -s_next))


def azimuth_div(q, v):
    cells = q.shape[1]

    def ahead(x):
        return pltpu.roll(x, cells - 1, 1)

    def behind(x):
        return pltpu.roll(x, 1, 1)

    q_next = ahead(q)
    step = q_next - q
    s = minmod(behind(step), step)
    flux = face_flux(q, q_next, s, ahead(s), v, ahead(v))
    return flux - behind(flux)


def kernel(
    split,
    tiles,
    rho_hbm,
    vr_hbm,
    va_hbm,
    coef_hbm,
    stop,
    gas_rho_hbm,
    gas_vr_hbm,
    gas_va_hbm,
    tiles_out,
    gas_out,
    tiles_in,
    gas_in,
    own_coef,
    mate_coef,
    q_rows,
    v_rows,
    a_rows,
    edge_send,
    edge_recv,
    adv,
    halves,
    all_bins,
    partial,
    partial_in,
    quad_sum,
    gas_rows,
    gain_send,
    gain_recv,
    load_sem,
    halo_send,
    halo_recv,
    give_send,
    item_recv,
    up_send,
    down_send,
    gain_send_sem,
    gain_recv_sem,
    coef_send,
    coef_recv,
    sum_send,
    sum_recv,
):
    xs, hs, ys, cores = split
    bins, cells = q_rows.shape[1:]
    half = cells // 2
    lane_tiles = cells // LANES
    t = lax.axis_index("tile")
    z = lax.axis_index("bin")
    core = t % cores
    y = (t // cores) % ys
    z_hi = (t // (cores * ys)) % hs
    x = t // (cores * ys * hs)
    w = z % QUAD
    quad = z // QUAD
    mate = (z + QUAD) % (2 * QUAD)
    own_base = quad * QUAD
    other_base = QUAD - own_base

    def tile_at(x_, y_, core_):
        return ((x_ * hs + z_hi) * ys + y_) * cores + core_

    def quad_at(i):
        return own_base + (w + i) % QUAD

    def lane_tile(l):
        return pl.ds(l * LANES, LANES)

    loads = [
        [
            pltpu.make_async_copy(src.at[:, lane_tile(l)], tiles_in.at[i, l], load_sem.at[i, l])
            for l in range(lane_tiles)
        ]
        for i, src in enumerate((rho_hbm, vr_hbm, va_hbm))
    ]
    load_coef = pltpu.make_async_copy(coef_hbm, own_coef, load_sem.at[3, 0])
    load_gas = [
        pltpu.make_async_copy(src, gas_in.at[i], load_sem.at[3, 1 + i])
        for i, src in enumerate((gas_rho_hbm, gas_vr_hbm, gas_va_hbm))
    ]
    for group in loads:
        for load in group:
            load.start()
    load_coef.start()
    for load in load_gas:
        load.start()

    barrier = pltpu.get_barrier_semaphore()
    peers = [(t, mate)] + [(t, quad_at(i)) for i in range(1, QUAD)]
    peers += [(tile_at(x, (y + i) % ys, core), z) for i in range(1, ys)]
    peers += [(tile_at((x + i) % xs, y, core), z) for i in range(1, xs)]
    peers += [((t + 1) % tiles, z), ((t + tiles - 1) % tiles, z)]
    for peer in peers:
        pl.semaphore_signal(barrier, inc=1, device_id=peer, device_id_type=MESH)

    has_prev = t > 0
    has_next = t < tiles - 1
    prev_dev = (jnp.maximum(t - 1, 0), z)
    next_dev = (jnp.minimum(t + 1, tiles - 1), z)

    stop_bin = lax.broadcasted_iota(jnp.int32, (bins, 1), 0)
    stop_col = jnp.zeros((bins, 1), F32)
    for b in range(bins):
        stop_col = jnp.where(stop_bin == b, stop[b], stop_col)
    couple = 1.0 / (1.0 + stop_col)
    keep = stop_col * couple

    partial[...] = jnp.zeros_like(partial)
    for group, rows, first in zip(loads, (q_rows, v_rows, a_rows), (2, 1, 0)):
        i = 2 - first
        for l, load in enumerate(group):
            load.wait()
            for r in range(ROWS):
                rows[first + r, :, lane_tile(l)] = tiles_in[i, l, pl.ds(r, bins, stride=ROWS), :]

    def put(i, r, value):
        for l in range(lane_tiles):
            tiles_out[i, l, pl.ds(r, bins, stride=ROWS), :] = value[:, l * LANES : (l + 1) * LANES]

    for i, (first, speed) in enumerate(((ROWS, ROWS), (2, 1))):
        edge_send[i, 0:2] = q_rows[first : first + 2].astype(BF16)
        edge_send[i, 2] = v_rows[speed].astype(BF16)

    pl.semaphore_wait(barrier, len(peers))

    def halo(i, device):
        return pltpu.make_async_remote_copy(
            src_ref=edge_send.at[i],
            dst_ref=edge_recv.at[i],
            send_sem=halo_send.at[i],
            recv_sem=halo_recv.at[i],
            device_id=device,
            device_id_type=MESH,
        )

    to_next, to_prev = halo(0, next_dev), halo(1, prev_dev)

    @pl.when(has_next)
    def _():
        to_next.start()

    @pl.when(has_prev)
    def _():
        to_prev.start()

    piece_rows = mate_coef.shape[3]
    piece = (core * xs + x) * ys + y

    def coef_copy(i, src, dst, device):
        return pltpu.make_async_remote_copy(
            src_ref=src,
            dst_ref=dst,
            send_sem=coef_send.at[i],
            recv_sem=coef_recv.at[i],
            device_id=device,
            device_id_type=MESH,
        )

    coef_from_mate = coef_copy(
        0,
        coef_hbm.at[pl.ds(pl.multiple_of(piece * piece_rows, piece_rows), piece_rows)],
        mate_coef.at[core, x, y],
        (t, mate),
    )
    coef_y = [
        coef_copy(i, mate_coef.at[core, x, y], mate_coef.at[core, x, y], (tile_at(x, (y + i) % ys, core), z))
        for i in range(1, ys)
    ]
    coef_x = [
        coef_copy(3 + i, mate_coef.at[core, x], mate_coef.at[core, x], (tile_at((x + i) % xs, y, core), z))
        for i in range(1, xs)
    ]
    coef_core = [
        coef_copy(6 + i, mate_coef.at[core], mate_coef.at[core], (tile_at(x, y, (core + i) % cores), z))
        for i in range(1, cores)
    ]

    def give(c):
        return pltpu.make_async_remote_copy(
            src_ref=halves.at[c, 1 - quad],
            dst_ref=all_bins.at[c, z],
            send_sem=give_send.at[c],
            recv_sem=item_recv.at[c, z],
            device_id=(t, mate),
            device_id_type=MESH,
        )

    def taken(c):
        return pltpu.make_async_remote_copy(
            src_ref=halves.at[c, 1 - quad],
            dst_ref=all_bins.at[c, mate],
            send_sem=give_send.at[c],
            recv_sem=item_recv.at[c, mate],
            device_id=(t, mate),
            device_id_type=MESH,
        )

    def pass_on(c, d, place, up):
        return pltpu.make_async_remote_copy(
            src_ref=all_bins.at[c, d],
            dst_ref=all_bins.at[c, d],
            send_sem=(up_send if up else down_send).at[place],
            recv_sem=item_recv.at[c, d],
            device_id=(t, jnp.minimum(z + 1, 2 * QUAD - 1) if up else jnp.maximum(z - 1, 0)),
            device_id_type=MESH,
        )

    can_up = w < QUAD - 1
    can_down = w > 0

    def send_both(c, d):
        @pl.when(can_up)
        def _():
            pass_on(c, d, w, True).start()

        @pl.when(can_down)
        def _():
            pass_on(c, d, w, False).start()

    def relay(c, far, base):
        @pl.when(w >= far)
        def _():
            place = jnp.maximum(w - far, 0)
            pass_on(c, base + place, place, True).wait_recv()
            if far < QUAD - 1:

                @pl.when(can_up)
                def _():
                    pass_on(c, base + place, place, True).start()

        @pl.when(w + far < QUAD)
        def _():
            place = jnp.minimum(w + far, QUAD - 1)
            pass_on(c, base + place, place, False).wait_recv()
            if far < QUAD - 1:

                @pl.when(can_down)
                def _():
                    pass_on(c, base + place, place, False).start()

    def own_relay(c, far):
        relay(c, far, own_base)

    def mate_relay(c, far):
        relay(c, far, other_base)

    def take_mates(c):
        taken(c).wait_recv()
        send_both(c, mate)

    def slope(i):
        return minmod(q_rows[i] - q_rows[i - 1], q_rows[i + 1] - q_rows[i])

    def radial_flux(r):
        return face_flux(
            q_rows[r + 1], q_rows[r + 2], slope(r + 1), slope(r + 2), v_rows[r], v_rows[r + 1]
        )

    def advect(c):
        before, last = None, None
        for j in range(DEEP):
            r = ROW_ORDER[DEEP * c + j]
            if last != r - 1:
                before = radial_flux(r)
            last = r
            after = radial_flux(r + 1)
            v_a = a_rows[r]
            q = q_rows[2 + r]
            new = q - COURANT * ((after - before) + azimuth_div(q, v_a))
            before = after
            adv[r] = new
            low = new.astype(BF16)
            halves[c, 0, j] = low[:, :half]
            halves[c, 1, j] = low[:, half:]
            weight = new * couple
            for n, term in enumerate((weight * v_rows[1 + r], weight * v_a, weight)):
                partial[r // 2, pl.ds(3 * (r % 2) + n, 1), :] = jnp.sum(term, axis=0, keepdims=True)

    def launch(c):
        all_bins[c, z] = halves[c, quad]
        give(c).start()
        send_both(c, z)

    def gains(c, coef, j):
        low = all_bins[c, :, j].reshape(2 * QUAD * bins, half)
        wide = low.astype(F32).reshape(1, 2 * QUAD * bins // 8, 8, half)
        inner = jnp.dot(coef, low, preferred_element_type=F32)
        terms = inner.reshape(bins, 2 * QUAD * bins // 8, 8, half) * wide
        return jnp.sum(jnp.sum(terms, axis=1), axis=1)

    def gain_copy(c):
        return pltpu.make_async_remote_copy(
            src_ref=gain_send.at[c],
            dst_ref=gain_recv.at[c],
            send_sem=gain_send_sem.at[c],
            recv_sem=gain_recv_sem.at[c],
            device_id=(t, mate),
            device_id_type=MESH,
        )

    def mate_gains(c):
        coef = mate_coef[...].reshape(own_coef.shape)
        for j in range(DEEP):
            gain_send[c, j] = gains(c, coef, j).astype(BF16)
        gain_copy(c).start()

    def own_gains(c):
        coef = own_coef[...]
        for j in range(DEEP):
            r = ROW_ORDER[DEEP * c + j]
            lanes = pl.ds(pl.multiple_of(quad * half, half), half)
            adv[r, :, lanes] = adv[r, :, lanes] + COAGULATION * gains(c, coef, j)

    def finish(c):
        gain_copy(c).wait_recv()
        for j in range(DEEP):
            r = ROW_ORDER[DEEP * c + j]
            lanes = pl.ds(pl.multiple_of((1 - quad) * half, half), half)
            adv[r, :, lanes] = adv[r, :, lanes] + COAGULATION * gain_recv[c, j].astype(F32)
            put(0, r, adv[r])

    def sum_copy(i, src, dst, device):
        return pltpu.make_async_remote_copy(
            src_ref=src,
            dst_ref=dst,
            send_sem=sum_send.at[i],
            recv_sem=sum_recv.at[i],
            device_id=device,
            device_id_type=MESH,
        )

    spread = [
        sum_copy(i, partial.at[(w + i) % QUAD], partial_in.at[i], (t, quad_at(i))) for i in range(1, QUAD)
    ]
    across = sum_copy(QUAD, quad_sum.at[0], quad_sum.at[1], (t, mate))
    shared = [
        sum_copy(QUAD + i, gas_rows.at[w], gas_rows.at[w], (t, quad_at(i))) for i in range(1, QUAD)
    ]
    shared_in = [
        sum_copy(QUAD + i, gas_rows.at[(w - i + QUAD) % QUAD], gas_rows.at[(w - i + QUAD) % QUAD], (t, quad_at(i)))
        for i in range(1, QUAD)
    ]

    def sum_across():
        total = partial[w]
        for copy in spread:
            copy.wait_recv()
        for i in range(1, QUAD):
            total = total + partial_in[i]
        quad_sum[0] = total
        across.start()

    def gas_step():
        for load in load_gas:
            load.wait()
        across.wait_recv()
        total = quad_sum[0] + quad_sum[1]
        for j in range(2):
            row = pl.ds(2 * w + j, 1)
            dense = gas_in[0, row, :]
            share = 1.0 / (dense + total[3 * j + 2 : 3 * j + 3])
            gas_rows[w, pl.ds(2 * j, 1), :] = (dense * gas_in[1, row, :] + total[3 * j : 3 * j + 1]) * share
            gas_rows[w, pl.ds(2 * j + 1, 1), :] = (dense * gas_in[2, row, :] + total[3 * j + 1 : 3 * j + 2]) * share
        for copy in shared:
            copy.start()

    def dust_speeds():
        for copy in shared_in:
            copy.wait_recv()
        for r in range(ROWS):
            u, j = r // 2, r % 2
            gas_r = gas_rows[u, pl.ds(2 * j, 1), :]
            gas_a = gas_rows[u, pl.ds(2 * j + 1, 1), :]
            gas_out[0, pl.ds(r, 1), :] = gas_r
            gas_out[1, pl.ds(r, 1), :] = gas_a
            put(1, r, v_rows[1 + r] * keep + gas_r * couple)
            put(2, r, a_rows[r] * keep + gas_a * couple)

    def halo_in():
        @pl.when(has_prev)
        def _():
            to_next.wait_recv()
            q_rows[0:2] = edge_recv[0, 0:2].astype(F32)
            v_rows[0] = edge_recv[0, 2].astype(F32)

        @pl.when(t == 0)
        def _():
            q_rows[0:2] = jnp.zeros_like(q_rows[0:2])
            v_rows[0] = jnp.zeros_like(v_rows[0])

        @pl.when(has_next)
        def _():
            to_prev.wait_recv()
            q_rows[ROWS + 2 : ROWS + 4] = edge_recv[1, 0:2].astype(F32)
            v_rows[ROWS + 1] = edge_recv[1, 2].astype(F32)

        @pl.when(t == tiles - 1)
        def _():
            q_rows[ROWS + 2 : ROWS + 4] = jnp.zeros_like(q_rows[0:2])
            v_rows[ROWS + 1] = jnp.zeros_like(v_rows[0])

    def start(copies):
        for copy in copies:
            copy.start()

    def receive(copies):
        for copy in copies:
            copy.wait_recv()

    coef_from_mate.start()
    advect(0)
    launch(0)
    coef_from_mate.wait_recv()
    start(coef_y)
    own_relay(0, 1)
    halo_in()
    advect(1)
    launch(1)
    start(spread)
    take_mates(0)
    own_relay(0, 2)
    receive(coef_y)
    start(coef_x)
    own_relay(1, 1)
    mate_relay(0, 1)
    sum_across()
    own_relay(1, 2)
    take_mates(1)
    mate_relay(0, 2)
    receive(coef_x)
    start(coef_core)
    mate_relay(1, 1)
    gas_step()
    load_coef.wait()
    own_relay(0, 3)
    mate_relay(0, 3)
    mate_relay(1, 2)
    own_gains(0)
    receive(coef_core)
    mate_gains(0)
    own_relay(1, 3)
    mate_relay(1, 3)
    mate_gains(1)
    dust_speeds()
    own_gains(1)
    for c in range(CHUNKS):
        finish(c)

    @pl.when(has_next)
    def _():
        to_next.wait_send()

    @pl.when(has_prev)
    def _():
        to_prev.wait_send()

    for copy in [coef_from_mate, across] + coef_y + coef_x + coef_core + spread + shared:
        copy.wait_send()
    for c in range(CHUNKS):
        give(c).wait_send()
        gain_copy(c).wait_send()
    for place in range(QUAD):
        for up in (True, False):

            @pl.when((can_up if up else can_down) & (place <= w if up else place >= w))
            def _():
                pltpu.make_async_remote_copy(
                    src_ref=all_bins.at[:, pl.ds(0, 2)],
                    dst_ref=all_bins.at[:, pl.ds(0, 2)],
                    send_sem=(up_send if up else down_send).at[place],
                    recv_sem=item_recv.at[0, 0],
                    device_id=(t, mate),
                    device_id_type=MESH,
                ).wait_send()


def write_out(tiles, gas, rho_out, vr_out, va_out, gas_vr_out, gas_va_out, sem, gas_sem):
    copies = [pltpu.make_async_copy(gas.at[i], out, gas_sem.at[i]) for i, out in enumerate((gas_vr_out, gas_va_out))]
    for i, out in enumerate((rho_out, vr_out, va_out)):
        for l in range(tiles.shape[1]):
            lanes = pl.ds(l * LANES, LANES)
            copies.append(pltpu.make_async_copy(tiles.at[i, l], out.at[:, lanes], sem.at[i, l]))
    for copy in copies:
        copy.start()
    for copy in copies:
        copy.wait()


def step(split, tiles, rho, vr, va, gas_rho, gas_vr, gas_va, stop, coef):
    bins, rows, cells = rho.shape
    half = cells // 2
    flat = (bins * rows, cells)
    total_bins = coef.shape[1]
    xs, _, ys, cores = split
    coef = coef.reshape(bins * total_bins, total_bins)
    dma = pltpu.SemaphoreType.DMA
    hbm = pl.BlockSpec(memory_space=pltpu.HBM)
    vmem = pl.BlockSpec(memory_space=pltpu.VMEM)
    lane_tiles = cells // LANES
    out_shape = [jax.ShapeDtypeStruct(flat, F32)] * 3 + [jax.ShapeDtypeStruct((rows, cells), F32)] * 2
    results = pl.pallas_call(
        functools.partial(kernel, split, tiles),
        out_shape=[
            jax.ShapeDtypeStruct((3, lane_tiles, flat[0], LANES), F32),
            jax.ShapeDtypeStruct((2, rows, cells), F32),
        ],
        in_specs=[hbm] * 4 + [pl.BlockSpec(memory_space=pltpu.SMEM)] + [hbm] * 3,
        out_specs=[vmem] * 2,
        scratch_shapes=[
            pltpu.VMEM((3, lane_tiles, flat[0], LANES), F32),
            pltpu.VMEM((3, rows, cells), F32),
            pltpu.VMEM(coef.shape, BF16),
            pltpu.VMEM((cores, xs, ys, coef.shape[0] // (cores * xs * ys), total_bins), BF16),
            pltpu.VMEM((rows + 4, bins, cells), F32),
            pltpu.VMEM((rows + 2, bins, cells), F32),
            pltpu.VMEM((rows, bins, cells), F32),
            pltpu.VMEM((2, 3, bins, cells), BF16),
            pltpu.VMEM((2, 3, bins, cells), BF16),
            pltpu.VMEM((rows, bins, cells), F32),
            pltpu.VMEM((CHUNKS, 2, DEEP, bins, half), BF16),
            pltpu.VMEM((CHUNKS, 2 * QUAD, DEEP, bins, half), BF16),
            pltpu.VMEM((QUAD, 8, cells), F32),
            pltpu.VMEM((QUAD, 8, cells), F32),
            pltpu.VMEM((2, 8, cells), F32),
            pltpu.VMEM((QUAD, 4, cells), F32),
            pltpu.VMEM((CHUNKS, DEEP, bins, half), BF16),
            pltpu.VMEM((CHUNKS, DEEP, bins, half), BF16),
            dma((4, lane_tiles)),
            dma((2,)),
            dma((2,)),
            dma((CHUNKS,)),
            dma((CHUNKS, 2 * QUAD)),
            dma((QUAD,)),
            dma((QUAD,)),
            dma((CHUNKS,)),
            dma((CHUNKS,)),
            dma((8,)),
            dma((8,)),
            dma((2 * QUAD,)),
            dma((2 * QUAD,)),
        ],
        compiler_params=pltpu.CompilerParams(
            collective_id=0, has_side_effects=True, vmem_limit_bytes=VMEM_BYTES
        ),
    )(
        *(pltpu.with_memory_space_constraint(x, pltpu.HBM) for x in (rho.reshape(flat), vr.reshape(flat), va.reshape(flat), coef)),
        stop,
        *(pltpu.with_memory_space_constraint(x, pltpu.HBM) for x in (gas_rho, gas_vr, gas_va)),
    )
    outs = pl.pallas_call(
        write_out,
        out_shape=out_shape,
        in_specs=[vmem] * 2,
        out_specs=[hbm] * 5,
        scratch_shapes=[dma((3, lane_tiles)), dma((2,))],
        compiler_params=pltpu.CompilerParams(vmem_limit_bytes=VMEM_BYTES),
    )(*results)
    return tuple(out.reshape(rho.shape) for out in outs[:3]) + tuple(outs[3:])


def solution(mesh):
    tiles = mesh.shape["tile"]
    grid = P("bin", "tile", None)
    gas = P("tile", None)
    return jax.shard_map(
        functools.partial(step, TILE_SPLIT[tiles], tiles),
        mesh=mesh,
        in_specs=(grid, grid, grid, gas, gas, gas, P("bin"), P("bin", None, None)),
        out_specs=(grid, grid, grid, gas, gas),
        check_vma=False,
    )
```

```python
import functools

import jax
import jax.numpy as jnp
from jax import lax
from jax.experimental import pallas as pl
from jax.experimental.pallas import tpu as pltpu
from jax.sharding import PartitionSpec as P

COURANT = 0.2
COAGULATION = 0.5
TILE_SPLIT = {128: (4, 4, 4, 2)}
QUAD = 4
ROWS = 8
LANES = 128
CHUNKS = 4
DEEP = ROWS // CHUNKS
VMEM_BYTES = 40 * 2**20
ROW_ORDER = (2, 3, 4, 5, 0, 1, 6, 7)
MESH = pl.DeviceIdType.MESH
F32 = jnp.float32
BF16 = jnp.bfloat16


def minmod(a, b):
    return jnp.maximum(jnp.minimum(a, b), 0.0) + jnp.minimum(jnp.maximum(a, b), 0.0)


def face_flux(q, q_next, s, s_next, v, v_next):
    u = 0.5 * (v + v_next)
    forward = u > 0
    reach = 0.5 - 0.5 * COURANT * jnp.abs(u)
    return u * (jnp.where(forward, q, q_next) + reach * jnp.where(forward, s, -s_next))


def azimuth_div(q, v):
    cells = q.shape[1]

    def ahead(x):
        return pltpu.roll(x, cells - 1, 1)

    def behind(x):
        return pltpu.roll(x, 1, 1)

    q_next = ahead(q)
    step = q_next - q
    s = minmod(behind(step), step)
    flux = face_flux(q, q_next, s, ahead(s), v, ahead(v))
    return flux - behind(flux)


def kernel(
    split,
    tiles,
    rho_hbm,
    vr_hbm,
    va_hbm,
    coef_hbm,
    stop_hbm,
    gas_rho_hbm,
    gas_vr_hbm,
    gas_va_hbm,
    tiles_out,
    gas_out,
    tiles_in,
    gas_in,
    stop,
    own_coef,
    mate_coef,
    q_rows,
    v_rows,
    a_rows,
    edge_send,
    edge_recv,
    adv,
    halves,
    all_bins,
    partial,
    partial_in,
    quad_sum,
    gas_rows,
    gain_send,
    gain_recv,
    load_sem,
    halo_send,
    halo_recv,
    give_send,
    item_recv,
    own_send,
    up_send,
    down_send,
    gain_send_sem,
    gain_recv_sem,
    coef_send,
    coef_recv,
    sum_send,
    sum_recv,
):
    xs, hs, ys, cores = split
    bins, cells = q_rows.shape[1:]
    half = cells // 2
    lane_tiles = cells // LANES
    t = lax.axis_index("tile")
    z = lax.axis_index("bin")
    core = t % cores
    y = (t // cores) % ys
    z_hi = (t // (cores * ys)) % hs
    x = t // (cores * ys * hs)
    w = z % QUAD
    quad = z // QUAD
    mate = (z + QUAD) % (2 * QUAD)
    own_base = quad * QUAD
    other_base = QUAD - own_base

    def tile_at(x_, y_, core_):
        return ((x_ * hs + z_hi) * ys + y_) * cores + core_

    def quad_at(i):
        return own_base + (w + i) % QUAD

    def lane_tile(l):
        return pl.ds(l * LANES, LANES)

    loads = [
        [
            pltpu.make_async_copy(src.at[:, lane_tile(l)], tiles_in.at[i, l], load_sem.at[i, l])
            for l in range(lane_tiles)
        ]
        for i, src in enumerate((rho_hbm, vr_hbm, va_hbm))
    ]
    load_coef = pltpu.make_async_copy(coef_hbm, own_coef, load_sem.at[3, 0])
    load_gas = [
        pltpu.make_async_copy(src, gas_in.at[i], load_sem.at[3, 1 + i])
        for i, src in enumerate((gas_rho_hbm, gas_vr_hbm, gas_va_hbm))
    ]
    load_stop = pltpu.make_async_copy(stop_hbm, stop, load_sem.at[4, 0])
    load_stop.start()
    for group in loads:
        for load in group:
            load.start()
    load_coef.start()
    for load in load_gas:
        load.start()

    barrier = pltpu.get_barrier_semaphore()
    peers = [(t, mate)] + [(t, quad_at(i)) for i in range(1, QUAD)]
    peers += [(tile_at(x, (y + i) % ys, core), z) for i in range(1, ys)]
    peers += [(tile_at((x + i) % xs, y, core), z) for i in range(1, xs)]
    peers += [((t + 1) % tiles, z), ((t + tiles - 1) % tiles, z)]
    for peer in peers:
        pl.semaphore_signal(barrier, inc=1, device_id=peer, device_id_type=MESH)

    has_prev = t > 0
    has_next = t < tiles - 1
    prev_dev = (jnp.maximum(t - 1, 0), z)
    next_dev = (jnp.minimum(t + 1, tiles - 1), z)

    load_stop.wait()
    stop_bin = lax.broadcasted_iota(jnp.int32, (bins, 1), 0)
    stop_col = jnp.zeros((bins, 1), F32)
    for b in range(bins):
        stop_col = jnp.where(stop_bin == b, stop[b], stop_col)
    couple = 1.0 / (1.0 + stop_col)
    keep = stop_col * couple

    partial[...] = jnp.zeros_like(partial)
    for group, rows, first in zip(loads, (q_rows, v_rows, a_rows), (2, 1, 0)):
        i = 2 - first
        for l, load in enumerate(group):
            load.wait()
            for r in range(ROWS):
                rows[first + r, :, lane_tile(l)] = tiles_in[i, l, pl.ds(r, bins, stride=ROWS), :]

    def put(i, r, value):
        for l in range(lane_tiles):
            tiles_out[i, l, pl.ds(r, bins, stride=ROWS), :] = value[:, l * LANES : (l + 1) * LANES]

    for i, (first, speed) in enumerate(((ROWS, ROWS), (2, 1))):
        edge_send[i, 0:2] = q_rows[first : first + 2].astype(BF16)
        edge_send[i, 2] = v_rows[speed].astype(BF16)

    pl.semaphore_wait(barrier, len(peers))

    def halo(i, device):
        return pltpu.make_async_remote_copy(
            src_ref=edge_send.at[i],
            dst_ref=edge_recv.at[i],
            send_sem=halo_send.at[i],
            recv_sem=halo_recv.at[i],
            device_id=device,
            device_id_type=MESH,
        )

    to_next, to_prev = halo(0, next_dev), halo(1, prev_dev)

    @pl.when(has_next)
    def _():
        to_next.start()

    @pl.when(has_prev)
    def _():
        to_prev.start()

    piece_rows = mate_coef.shape[3]
    piece = (core * xs + x) * ys + y

    def coef_copy(i, src, dst, device):
        return pltpu.make_async_remote_copy(
            src_ref=src,
            dst_ref=dst,
            send_sem=coef_send.at[i],
            recv_sem=coef_recv.at[i],
            device_id=device,
            device_id_type=MESH,
        )

    coef_from_mate = coef_copy(
        0,
        coef_hbm.at[pl.ds(pl.multiple_of(piece * piece_rows, piece_rows), piece_rows)],
        mate_coef.at[core, x, y],
        (t, mate),
    )
    coef_y = [
        coef_copy(i, mate_coef.at[core, x, y], mate_coef.at[core, x, y], (tile_at(x, (y + i) % ys, core), z))
        for i in range(1, ys)
    ]
    coef_x = [
        coef_copy(3 + i, mate_coef.at[core, x], mate_coef.at[core, x], (tile_at((x + i) % xs, y, core), z))
        for i in range(1, xs)
    ]
    coef_core = [
        coef_copy(6 + i, mate_coef.at[core], mate_coef.at[core], (tile_at(x, y, (core + i) % cores), z))
        for i in range(1, cores)
    ]

    def give(c):
        return pltpu.make_async_remote_copy(
            src_ref=halves.at[c, 1 - quad],
            dst_ref=all_bins.at[c, z],
            send_sem=give_send.at[c],
            recv_sem=item_recv.at[c, z],
            device_id=(t, mate),
            device_id_type=MESH,
        )

    def taken(c):
        return pltpu.make_async_remote_copy(
            src_ref=halves.at[c, 1 - quad],
            dst_ref=all_bins.at[c, mate],
            send_sem=give_send.at[c],
            recv_sem=item_recv.at[c, mate],
            device_id=(t, mate),
            device_id_type=MESH,
        )

    def pass_on(c, d, place, up):
        return pltpu.make_async_remote_copy(
            src_ref=all_bins.at[c, d],
            dst_ref=all_bins.at[c, d],
            send_sem=(up_send if up else down_send).at[place],
            recv_sem=item_recv.at[c, d],
            device_id=(t, jnp.minimum(z + 1, 2 * QUAD - 1) if up else jnp.maximum(z - 1, 0)),
            device_id_type=MESH,
        )

    can_up = w < QUAD - 1
    can_down = w > 0

    def send_both(c, d):
        @pl.when(can_up)
        def _():
            pass_on(c, d, w, True).start()

        @pl.when(can_down)
        def _():
            pass_on(c, d, w, False).start()

    def relay(c, far, base):
        @pl.when(w >= far)
        def _():
            place = jnp.maximum(w - far, 0)
            pass_on(c, base + place, place, True).wait_recv()
            if far < QUAD - 1:

                @pl.when(can_up)
                def _():
                    pass_on(c, base + place, place, True).start()

        @pl.when(w + far < QUAD)
        def _():
            place = jnp.minimum(w + far, QUAD - 1)
            pass_on(c, base + place, place, False).wait_recv()
            if far < QUAD - 1:

                @pl.when(can_down)
                def _():
                    pass_on(c, base + place, place, False).start()

    def own_items(c):
        return [
            pltpu.make_async_remote_copy(
                src_ref=all_bins.at[c, z],
                dst_ref=all_bins.at[c, z],
                send_sem=own_send.at[c, i],
                recv_sem=item_recv.at[c, z],
                device_id=(t, quad_at(i)),
                device_id_type=MESH,
            )
            for i in range(1, QUAD)
        ]

    def own_receive(c):
        for i in range(1, QUAD):
            pltpu.make_async_remote_copy(
                src_ref=all_bins.at[c, quad_at(i)],
                dst_ref=all_bins.at[c, quad_at(i)],
                send_sem=own_send.at[c, i],
                recv_sem=item_recv.at[c, quad_at(i)],
                device_id=(t, quad_at(i)),
                device_id_type=MESH,
            ).wait_recv()

    def mate_relay(c, far):
        relay(c, far, other_base)

    def take_mates(c):
        taken(c).wait_recv()
        send_both(c, mate)

    def slope(i):
        return minmod(q_rows[i] - q_rows[i - 1], q_rows[i + 1] - q_rows[i])

    def radial_flux(r):
        return face_flux(
            q_rows[r + 1], q_rows[r + 2], slope(r + 1), slope(r + 2), v_rows[r], v_rows[r + 1]
        )

    def advect(c):
        before, last = None, None
        for j in range(DEEP):
            r = ROW_ORDER[DEEP * c + j]
            if last != r - 1:
                before = radial_flux(r)
            last = r
            after = radial_flux(r + 1)
            v_a = a_rows[r]
            q = q_rows[2 + r]
            new = q - COURANT * ((after - before) + azimuth_div(q, v_a))
            before = after
            adv[r] = new
            low = new.astype(BF16)
            halves[c, 0, j] = low[:, :half]
            halves[c, 1, j] = low[:, half:]
            weight = new * couple
            for n, term in enumerate((weight * v_rows[1 + r], weight * v_a, weight)):
                partial[r // 2, pl.ds(3 * (r % 2) + n, 1), :] = jnp.sum(term, axis=0, keepdims=True)

    def launch(c):
        all_bins[c, z] = halves[c, quad]
        give(c).start()
        for copy in own_items(c):
            copy.start()

    def gains(c, coef, j):
        low = all_bins[c, :, j].reshape(2 * QUAD * bins, half)
        wide = low.astype(F32).reshape(1, 2 * QUAD * bins // 8, 8, half)
        inner = jnp.dot(coef, low, preferred_element_type=F32)
        terms = inner.reshape(bins, 2 * QUAD * bins // 8, 8, half) * wide
        return jnp.sum(jnp.sum(terms, axis=1), axis=1)

    def gain_copy(c):
        return pltpu.make_async_remote_copy(
            src_ref=gain_send.at[c],
            dst_ref=gain_recv.at[c],
            send_sem=gain_send_sem.at[c],
            recv_sem=gain_recv_sem.at[c],
            device_id=(t, mate),
            device_id_type=MESH,
        )

    def mate_gains(c):
        coef = mate_coef[...].reshape(own_coef.shape)
        for j in range(DEEP):
            gain_send[c, j] = gains(c, coef, j).astype(BF16)
        gain_copy(c).start()

    def own_gains(c):
        coef = own_coef[...]
        for j in range(DEEP):
            r = ROW_ORDER[DEEP * c + j]
            lanes = pl.ds(pl.multiple_of(quad * half, half), half)
            adv[r, :, lanes] = adv[r, :, lanes] + COAGULATION * gains(c, coef, j)

    def finish(c):
        gain_copy(c).wait_recv()
        for j in range(DEEP):
            r = ROW_ORDER[DEEP * c + j]
            lanes = pl.ds(pl.multiple_of((1 - quad) * half, half), half)
            adv[r, :, lanes] = adv[r, :, lanes] + COAGULATION * gain_recv[c, j].astype(F32)
            put(0, r, adv[r])

    def sum_copy(i, src, dst, device):
        return pltpu.make_async_remote_copy(
            src_ref=src,
            dst_ref=dst,
            send_sem=sum_send.at[i],
            recv_sem=sum_recv.at[i],
            device_id=device,
            device_id_type=MESH,
        )

    spread = [
        sum_copy(i, partial.at[(w + i) % QUAD], partial_in.at[i], (t, quad_at(i))) for i in range(1, QUAD)
    ]
    across = sum_copy(QUAD, quad_sum.at[0], quad_sum.at[1], (t, mate))
    shared = [
        sum_copy(QUAD + i, gas_rows.at[w], gas_rows.at[w], (t, quad_at(i))) for i in range(1, QUAD)
    ]
    shared_in = [
        sum_copy(QUAD + i, gas_rows.at[(w - i + QUAD) % QUAD], gas_rows.at[(w - i + QUAD) % QUAD], (t, quad_at(i)))
        for i in range(1, QUAD)
    ]

    def sum_across():
        total = partial[w]
        for copy in spread:
            copy.wait_recv()
        for i in range(1, QUAD):
            total = total + partial_in[i]
        quad_sum[0] = total
        across.start()

    def gas_step():
        for load in load_gas:
            load.wait()
        across.wait_recv()
        total = quad_sum[0] + quad_sum[1]
        for j in range(2):
            row = pl.ds(2 * w + j, 1)
            dense = gas_in[0, row, :]
            share = 1.0 / (dense + total[3 * j + 2 : 3 * j + 3])
            gas_rows[w, pl.ds(2 * j, 1), :] = (dense * gas_in[1, row, :] + total[3 * j : 3 * j + 1]) * share
            gas_rows[w, pl.ds(2 * j + 1, 1), :] = (dense * gas_in[2, row, :] + total[3 * j + 1 : 3 * j + 2]) * share
        for copy in shared:
            copy.start()

    def dust_speeds():
        for copy in shared_in:
            copy.wait_recv()
        for r in range(ROWS):
            u, j = r // 2, r % 2
            gas_r = gas_rows[u, pl.ds(2 * j, 1), :]
            gas_a = gas_rows[u, pl.ds(2 * j + 1, 1), :]
            gas_out[0, pl.ds(r, 1), :] = gas_r
            gas_out[1, pl.ds(r, 1), :] = gas_a
            put(1, r, v_rows[1 + r] * keep + gas_r * couple)
            put(2, r, a_rows[r] * keep + gas_a * couple)

    def halo_in():
        @pl.when(has_prev)
        def _():
            to_next.wait_recv()
            q_rows[0:2] = edge_recv[0, 0:2].astype(F32)
            v_rows[0] = edge_recv[0, 2].astype(F32)

        @pl.when(t == 0)
        def _():
            q_rows[0:2] = jnp.zeros_like(q_rows[0:2])
            v_rows[0] = jnp.zeros_like(v_rows[0])

        @pl.when(has_next)
        def _():
            to_prev.wait_recv()
            q_rows[ROWS + 2 : ROWS + 4] = edge_recv[1, 0:2].astype(F32)
            v_rows[ROWS + 1] = edge_recv[1, 2].astype(F32)

        @pl.when(t == tiles - 1)
        def _():
            q_rows[ROWS + 2 : ROWS + 4] = jnp.zeros_like(q_rows[0:2])
            v_rows[ROWS + 1] = jnp.zeros_like(v_rows[0])

    def start(copies):
        for copy in copies:
            copy.start()

    def receive(copies):
        for copy in copies:
            copy.wait_recv()

    coef_from_mate.start()
    advect(0)
    launch(0)
    advect(1)
    launch(1)
    coef_from_mate.wait_recv()
    start(coef_y)
    halo_in()
    advect(2)
    launch(2)
    advect(3)
    launch(3)
    start(spread)
    take_mates(0)
    receive(coef_y)
    start(coef_x)
    take_mates(1)
    mate_relay(0, 1)
    sum_across()
    mate_relay(1, 1)
    take_mates(2)
    mate_relay(0, 2)
    take_mates(3)
    mate_relay(1, 2)
    mate_relay(2, 1)
    receive(coef_x)
    start(coef_core)
    mate_relay(3, 1)
    gas_step()
    load_coef.wait()
    own_receive(0)
    mate_relay(0, 3)
    mate_relay(2, 2)
    own_gains(0)
    mate_relay(3, 2)
    receive(coef_core)
    mate_gains(0)
    own_receive(1)
    mate_relay(1, 3)
    mate_gains(1)
    own_receive(2)
    mate_relay(2, 3)
    mate_gains(2)
    own_receive(3)
    mate_relay(3, 3)
    mate_gains(3)
    own_gains(1)
    own_gains(2)
    dust_speeds()
    own_gains(3)
    for c in range(CHUNKS):
        finish(c)

    @pl.when(has_next)
    def _():
        to_next.wait_send()

    @pl.when(has_prev)
    def _():
        to_prev.wait_send()

    for copy in [coef_from_mate, across] + coef_y + coef_x + coef_core + spread + shared:
        copy.wait_send()
    for c in range(CHUNKS):
        give(c).wait_send()
        for copy in own_items(c):
            copy.wait_send()
        gain_copy(c).wait_send()
    for place in range(QUAD):
        for up in (True, False):

            @pl.when((can_up if up else can_down) & (place <= w if up else place >= w))
            def _():
                pltpu.make_async_remote_copy(
                    src_ref=all_bins.at[:, pl.ds(0, 1)],
                    dst_ref=all_bins.at[:, pl.ds(0, 1)],
                    send_sem=(up_send if up else down_send).at[place],
                    recv_sem=item_recv.at[0, 0],
                    device_id=(t, mate),
                    device_id_type=MESH,
                ).wait_send()


def write_out(tiles, gas, rho_out, vr_out, va_out, gas_vr_out, gas_va_out, sem, gas_sem):
    copies = [pltpu.make_async_copy(gas.at[i], out, gas_sem.at[i]) for i, out in enumerate((gas_vr_out, gas_va_out))]
    for i, out in enumerate((rho_out, vr_out, va_out)):
        for l in range(tiles.shape[1]):
            lanes = pl.ds(l * LANES, LANES)
            copies.append(pltpu.make_async_copy(tiles.at[i, l], out.at[:, lanes], sem.at[i, l]))
    for copy in copies:
        copy.start()
    for copy in copies:
        copy.wait()


def step(split, tiles, rho, vr, va, gas_rho, gas_vr, gas_va, stop, coef):
    bins, rows, cells = rho.shape
    half = cells // 2
    flat = (bins * rows, cells)
    total_bins = coef.shape[1]
    xs, _, ys, cores = split
    coef = coef.reshape(bins * total_bins, total_bins)
    dma = pltpu.SemaphoreType.DMA
    hbm = pl.BlockSpec(memory_space=pltpu.HBM)
    vmem = pl.BlockSpec(memory_space=pltpu.VMEM)
    lane_tiles = cells // LANES
    out_shape = [jax.ShapeDtypeStruct(flat, F32)] * 3 + [jax.ShapeDtypeStruct((rows, cells), F32)] * 2
    results = pl.pallas_call(
        functools.partial(kernel, split, tiles),
        out_shape=[
            jax.ShapeDtypeStruct((3, lane_tiles, flat[0], LANES), F32),
            jax.ShapeDtypeStruct((2, rows, cells), F32),
        ],
        in_specs=[hbm] * 8,
        out_specs=[vmem] * 2,
        scratch_shapes=[
            pltpu.VMEM((3, lane_tiles, flat[0], LANES), F32),
            pltpu.VMEM((3, rows, cells), F32),
            pltpu.SMEM((bins,), F32),
            pltpu.VMEM(coef.shape, BF16),
            pltpu.VMEM((cores, xs, ys, coef.shape[0] // (cores * xs * ys), total_bins), BF16),
            pltpu.VMEM((rows + 4, bins, cells), F32),
            pltpu.VMEM((rows + 2, bins, cells), F32),
            pltpu.VMEM((rows, bins, cells), F32),
            pltpu.VMEM((2, 3, bins, cells), BF16),
            pltpu.VMEM((2, 3, bins, cells), BF16),
            pltpu.VMEM((rows, bins, cells), F32),
            pltpu.VMEM((CHUNKS, 2, DEEP, bins, half), BF16),
            pltpu.VMEM((CHUNKS, 2 * QUAD, DEEP, bins, half), BF16),
            pltpu.VMEM((QUAD, 8, cells), F32),
            pltpu.VMEM((QUAD, 8, cells), F32),
            pltpu.VMEM((2, 8, cells), F32),
            pltpu.VMEM((QUAD, 4, cells), F32),
            pltpu.VMEM((CHUNKS, DEEP, bins, half), BF16),
            pltpu.VMEM((CHUNKS, DEEP, bins, half), BF16),
            dma((5, lane_tiles)),
            dma((2,)),
            dma((2,)),
            dma((CHUNKS,)),
            dma((CHUNKS, 2 * QUAD)),
            dma((CHUNKS, QUAD)),
            dma((QUAD,)),
            dma((QUAD,)),
            dma((CHUNKS,)),
            dma((CHUNKS,)),
            dma((8,)),
            dma((8,)),
            dma((2 * QUAD,)),
            dma((2 * QUAD,)),
        ],
        compiler_params=pltpu.CompilerParams(
            collective_id=0, has_side_effects=True, vmem_limit_bytes=VMEM_BYTES
        ),
    )(
        *(
            pltpu.with_memory_space_constraint(x, pltpu.HBM)
            for x in (rho.reshape(flat), vr.reshape(flat), va.reshape(flat), coef, stop, gas_rho, gas_vr, gas_va)
        )
    )
    outs = pl.pallas_call(
        write_out,
        out_shape=out_shape,
        in_specs=[vmem] * 2,
        out_specs=[hbm] * 5,
        scratch_shapes=[dma((3, lane_tiles)), dma((2,))],
        compiler_params=pltpu.CompilerParams(vmem_limit_bytes=VMEM_BYTES),
    )(*results)
    return tuple(out.reshape(rho.shape) for out in outs[:3]) + tuple(outs[3:])


def solution(mesh):
    tiles = mesh.shape["tile"]
    grid = P("bin", "tile", None)
    gas = P("tile", None)
    return jax.shard_map(
        functools.partial(step, TILE_SPLIT[tiles], tiles),
        mesh=mesh,
        in_specs=(grid, grid, grid, gas, gas, gas, P("bin"), P("bin", None, None)),
        out_specs=(grid, grid, grid, gas, gas),
        check_vma=False,
    )
```

```python
import functools

import jax
import jax.numpy as jnp
from jax import lax
from jax.experimental import pallas as pl
from jax.experimental.pallas import tpu as pltpu
from jax.sharding import PartitionSpec as P

COURANT = 0.2
COAGULATION = 0.5
TILE_SPLIT = {128: (4, 4, 4, 2)}
QUAD = 4
ROWS = 8
LANES = 128
CHUNKS = 4
DEEP = ROWS // CHUNKS
VMEM_BYTES = 40 * 2**20
ROW_ORDER = (2, 3, 4, 5, 0, 1, 6, 7)
MESH = pl.DeviceIdType.MESH
F32 = jnp.float32
BF16 = jnp.bfloat16


def minmod(a, b):
    return jnp.maximum(jnp.minimum(a, b), 0.0) + jnp.minimum(jnp.maximum(a, b), 0.0)


def face_flux(q, q_next, s, s_next, v, v_next):
    u = 0.5 * (v + v_next)
    forward = u > 0
    reach = 0.5 - 0.5 * COURANT * jnp.abs(u)
    return u * (jnp.where(forward, q, q_next) + reach * jnp.where(forward, s, -s_next))


def azimuth_div(q, v):
    cells = q.shape[1]

    def ahead(x):
        return pltpu.roll(x, cells - 1, 1)

    def behind(x):
        return pltpu.roll(x, 1, 1)

    q_next = ahead(q)
    step = q_next - q
    s = minmod(behind(step), step)
    flux = face_flux(q, q_next, s, ahead(s), v, ahead(v))
    return flux - behind(flux)


def kernel(
    split,
    tiles,
    rho_hbm,
    vr_hbm,
    va_hbm,
    coef_hbm,
    stop_hbm,
    gas_rho_hbm,
    gas_vr_hbm,
    gas_va_hbm,
    tiles_out,
    gas_out,
    tiles_in,
    gas_in,
    stop,
    own_coef,
    mate_coef,
    q_rows,
    v_rows,
    a_rows,
    edge_send,
    edge_recv,
    adv,
    halves,
    all_bins,
    partial,
    partial_in,
    quad_sum,
    gas_rows,
    gain_send,
    gain_recv,
    load_sem,
    halo_send,
    halo_recv,
    give_send,
    item_recv,
    own_send,
    up_send,
    down_send,
    gain_send_sem,
    gain_recv_sem,
    coef_send,
    coef_recv,
    sum_send,
    sum_recv,
):
    xs, hs, ys, cores = split
    bins, cells = q_rows.shape[1:]
    half = cells // 2
    lane_tiles = cells // LANES
    t = lax.axis_index("tile")
    z = lax.axis_index("bin")
    core = t % cores
    y = (t // cores) % ys
    z_hi = (t // (cores * ys)) % hs
    x = t // (cores * ys * hs)
    w = z % QUAD
    quad = z // QUAD
    mate = (z + QUAD) % (2 * QUAD)
    own_base = quad * QUAD
    other_base = QUAD - own_base

    def tile_at(x_, y_, core_):
        return ((x_ * hs + z_hi) * ys + y_) * cores + core_

    def quad_at(i):
        return own_base + (w + i) % QUAD

    def lane_tile(l):
        return pl.ds(l * LANES, LANES)

    loads = [
        [
            pltpu.make_async_copy(src.at[:, lane_tile(l)], tiles_in.at[i, l], load_sem.at[i, l])
            for l in range(lane_tiles)
        ]
        for i, src in enumerate((rho_hbm, vr_hbm, va_hbm))
    ]
    load_coef = pltpu.make_async_copy(coef_hbm, own_coef, load_sem.at[3, 0])
    load_gas = [
        pltpu.make_async_copy(src, gas_in.at[i], load_sem.at[3, 1 + i])
        for i, src in enumerate((gas_rho_hbm, gas_vr_hbm, gas_va_hbm))
    ]
    load_stop = pltpu.make_async_copy(stop_hbm, stop, load_sem.at[4, 0])
    load_stop.start()
    for group in loads:
        for load in group:
            load.start()
    load_coef.start()
    for load in load_gas:
        load.start()

    barrier = pltpu.get_barrier_semaphore()
    peers = [(t, mate)] + [(t, quad_at(i)) for i in range(1, QUAD)]
    peers += [(tile_at(x, (y + i) % ys, core), z) for i in range(1, ys)]
    peers += [(tile_at((x + i) % xs, y, core), z) for i in range(1, xs)]
    peers += [((t + 1) % tiles, z), ((t + tiles - 1) % tiles, z)]
    for peer in peers:
        pl.semaphore_signal(barrier, inc=1, device_id=peer, device_id_type=MESH)

    has_prev = t > 0
    has_next = t < tiles - 1
    prev_dev = (jnp.maximum(t - 1, 0), z)
    next_dev = (jnp.minimum(t + 1, tiles - 1), z)

    load_stop.wait()
    stop_bin = lax.broadcasted_iota(jnp.int32, (bins, 1), 0)
    stop_col = jnp.zeros((bins, 1), F32)
    for b in range(bins):
        stop_col = jnp.where(stop_bin == b, stop[b], stop_col)
    couple = 1.0 / (1.0 + stop_col)
    keep = stop_col * couple

    partial[...] = jnp.zeros_like(partial)

    def unpack(i, rows, first):
        for l, load in enumerate(loads[i]):
            load.wait()
            for r in range(ROWS):
                rows[first + r, :, lane_tile(l)] = tiles_in[i, l, pl.ds(r, bins, stride=ROWS), :]

    unpack(0, q_rows, 2)
    unpack(1, v_rows, 1)

    def put(i, r, value):
        for l in range(lane_tiles):
            tiles_out[i, l, pl.ds(r, bins, stride=ROWS), :] = value[:, l * LANES : (l + 1) * LANES]

    for i, (first, speed) in enumerate(((ROWS, ROWS), (2, 1))):
        edge_send[i, 0:2] = q_rows[first : first + 2].astype(BF16)
        edge_send[i, 2] = v_rows[speed].astype(BF16)

    pl.semaphore_wait(barrier, len(peers))

    def halo(i, device):
        return pltpu.make_async_remote_copy(
            src_ref=edge_send.at[i],
            dst_ref=edge_recv.at[i],
            send_sem=halo_send.at[i],
            recv_sem=halo_recv.at[i],
            device_id=device,
            device_id_type=MESH,
        )

    to_next, to_prev = halo(0, next_dev), halo(1, prev_dev)

    @pl.when(has_next)
    def _():
        to_next.start()

    @pl.when(has_prev)
    def _():
        to_prev.start()

    piece_rows = mate_coef.shape[3]
    piece = (core * xs + x) * ys + y

    def coef_copy(i, src, dst, device):
        return pltpu.make_async_remote_copy(
            src_ref=src,
            dst_ref=dst,
            send_sem=coef_send.at[i],
            recv_sem=coef_recv.at[i],
            device_id=device,
            device_id_type=MESH,
        )

    coef_from_mate = coef_copy(
        0,
        coef_hbm.at[pl.ds(pl.multiple_of(piece * piece_rows, piece_rows), piece_rows)],
        mate_coef.at[core, x, y],
        (t, mate),
    )
    coef_y = [
        coef_copy(i, mate_coef.at[core, x, y], mate_coef.at[core, x, y], (tile_at(x, (y + i) % ys, core), z))
        for i in range(1, ys)
    ]
    coef_x = [
        coef_copy(3 + i, mate_coef.at[core, x], mate_coef.at[core, x], (tile_at((x + i) % xs, y, core), z))
        for i in range(1, xs)
    ]
    coef_core = [
        coef_copy(6 + i, mate_coef.at[core], mate_coef.at[core], (tile_at(x, y, (core + i) % cores), z))
        for i in range(1, cores)
    ]

    def give(c):
        return pltpu.make_async_remote_copy(
            src_ref=halves.at[c, 1 - quad],
            dst_ref=all_bins.at[c, z],
            send_sem=give_send.at[c],
            recv_sem=item_recv.at[c, z],
            device_id=(t, mate),
            device_id_type=MESH,
        )

    def taken(c):
        return pltpu.make_async_remote_copy(
            src_ref=halves.at[c, 1 - quad],
            dst_ref=all_bins.at[c, mate],
            send_sem=give_send.at[c],
            recv_sem=item_recv.at[c, mate],
            device_id=(t, mate),
            device_id_type=MESH,
        )

    def pass_on(c, d, place, up):
        return pltpu.make_async_remote_copy(
            src_ref=all_bins.at[c, d],
            dst_ref=all_bins.at[c, d],
            send_sem=(up_send if up else down_send).at[place],
            recv_sem=item_recv.at[c, d],
            device_id=(t, jnp.minimum(z + 1, 2 * QUAD - 1) if up else jnp.maximum(z - 1, 0)),
            device_id_type=MESH,
        )

    can_up = w < QUAD - 1
    can_down = w > 0

    def send_both(c, d):
        @pl.when(can_up)
        def _():
            pass_on(c, d, w, True).start()

        @pl.when(can_down)
        def _():
            pass_on(c, d, w, False).start()

    def relay(c, far, base):
        @pl.when(w >= far)
        def _():
            place = jnp.maximum(w - far, 0)
            pass_on(c, base + place, place, True).wait_recv()
            if far < QUAD - 1:

                @pl.when(can_up)
                def _():
                    pass_on(c, base + place, place, True).start()

        @pl.when(w + far < QUAD)
        def _():
            place = jnp.minimum(w + far, QUAD - 1)
            pass_on(c, base + place, place, False).wait_recv()
            if far < QUAD - 1:

                @pl.when(can_down)
                def _():
                    pass_on(c, base + place, place, False).start()

    def own_items(c):
        return [
            pltpu.make_async_remote_copy(
                src_ref=all_bins.at[c, z],
                dst_ref=all_bins.at[c, z],
                send_sem=own_send.at[c, i],
                recv_sem=item_recv.at[c, z],
                device_id=(t, quad_at(i)),
                device_id_type=MESH,
            )
            for i in range(1, QUAD)
        ]

    def own_receive(c):
        for i in range(1, QUAD):
            pltpu.make_async_remote_copy(
                src_ref=all_bins.at[c, quad_at(i)],
                dst_ref=all_bins.at[c, quad_at(i)],
                send_sem=own_send.at[c, i],
                recv_sem=item_recv.at[c, quad_at(i)],
                device_id=(t, quad_at(i)),
                device_id_type=MESH,
            ).wait_recv()

    def mate_relay(c, far):
        relay(c, far, other_base)

    def take_mates(c):
        taken(c).wait_recv()
        send_both(c, mate)

    def slope(i):
        return minmod(q_rows[i] - q_rows[i - 1], q_rows[i + 1] - q_rows[i])

    def radial_flux(r):
        return face_flux(
            q_rows[r + 1], q_rows[r + 2], slope(r + 1), slope(r + 2), v_rows[r], v_rows[r + 1]
        )

    def advect(c):
        before, last = None, None
        for j in range(DEEP):
            r = ROW_ORDER[DEEP * c + j]
            if last != r - 1:
                before = radial_flux(r)
            last = r
            after = radial_flux(r + 1)
            v_a = a_rows[r]
            q = q_rows[2 + r]
            new = q - COURANT * ((after - before) + azimuth_div(q, v_a))
            before = after
            adv[r] = new
            low = new.astype(BF16)
            halves[c, 0, j] = low[:, :half]
            halves[c, 1, j] = low[:, half:]
            weight = new * couple
            for n, term in enumerate((weight * v_rows[1 + r], weight * v_a, weight)):
                partial[r // 2, pl.ds(3 * (r % 2) + n, 1), :] = jnp.sum(term, axis=0, keepdims=True)

    def launch(c):
        all_bins[c, z] = halves[c, quad]
        give(c).start()
        for copy in own_items(c):
            copy.start()

    def gains(c, coef, j):
        low = all_bins[c, :, j].reshape(2 * QUAD * bins, half)
        wide = low.astype(F32).reshape(1, 2 * QUAD * bins // 8, 8, half)
        inner = jnp.dot(coef, low, preferred_element_type=F32)
        terms = inner.reshape(bins, 2 * QUAD * bins // 8, 8, half) * wide
        return jnp.sum(jnp.sum(terms, axis=1), axis=1)

    def gain_copy(c):
        return pltpu.make_async_remote_copy(
            src_ref=gain_send.at[c],
            dst_ref=gain_recv.at[c],
            send_sem=gain_send_sem.at[c],
            recv_sem=gain_recv_sem.at[c],
            device_id=(t, mate),
            device_id_type=MESH,
        )

    def mate_gains(c):
        coef = mate_coef[...].reshape(own_coef.shape)
        for j in range(DEEP):
            gain_send[c, j] = gains(c, coef, j).astype(BF16)
        gain_copy(c).start()

    def own_gains(c):
        coef = own_coef[...]
        for j in range(DEEP):
            r = ROW_ORDER[DEEP * c + j]
            lanes = pl.ds(pl.multiple_of(quad * half, half), half)
            adv[r, :, lanes] = adv[r, :, lanes] + COAGULATION * gains(c, coef, j)

    def finish(c):
        gain_copy(c).wait_recv()
        for j in range(DEEP):
            r = ROW_ORDER[DEEP * c + j]
            lanes = pl.ds(pl.multiple_of((1 - quad) * half, half), half)
            adv[r, :, lanes] = adv[r, :, lanes] + COAGULATION * gain_recv[c, j].astype(F32)
            put(0, r, adv[r])

    def sum_copy(i, src, dst, device):
        return pltpu.make_async_remote_copy(
            src_ref=src,
            dst_ref=dst,
            send_sem=sum_send.at[i],
            recv_sem=sum_recv.at[i],
            device_id=device,
            device_id_type=MESH,
        )

    spread = [
        sum_copy(i, partial.at[(w + i) % QUAD], partial_in.at[i], (t, quad_at(i))) for i in range(1, QUAD)
    ]
    across = sum_copy(QUAD, quad_sum.at[0], quad_sum.at[1], (t, mate))
    shared = [
        sum_copy(QUAD + i, gas_rows.at[w], gas_rows.at[w], (t, quad_at(i))) for i in range(1, QUAD)
    ]
    shared_in = [
        sum_copy(QUAD + i, gas_rows.at[(w - i + QUAD) % QUAD], gas_rows.at[(w - i + QUAD) % QUAD], (t, quad_at(i)))
        for i in range(1, QUAD)
    ]

    def sum_across():
        total = partial[w]
        for copy in spread:
            copy.wait_recv()
        for i in range(1, QUAD):
            total = total + partial_in[i]
        quad_sum[0] = total
        across.start()

    def gas_step():
        for load in load_gas:
            load.wait()
        across.wait_recv()
        total = quad_sum[0] + quad_sum[1]
        for j in range(2):
            row = pl.ds(2 * w + j, 1)
            dense = gas_in[0, row, :]
            share = 1.0 / (dense + total[3 * j + 2 : 3 * j + 3])
            gas_rows[w, pl.ds(2 * j, 1), :] = (dense * gas_in[1, row, :] + total[3 * j : 3 * j + 1]) * share
            gas_rows[w, pl.ds(2 * j + 1, 1), :] = (dense * gas_in[2, row, :] + total[3 * j + 1 : 3 * j + 2]) * share
        for copy in shared:
            copy.start()

    def dust_speeds():
        for copy in shared_in:
            copy.wait_recv()
        for r in range(ROWS):
            u, j = r // 2, r % 2
            gas_r = gas_rows[u, pl.ds(2 * j, 1), :]
            gas_a = gas_rows[u, pl.ds(2 * j + 1, 1), :]
            gas_out[0, pl.ds(r, 1), :] = gas_r
            gas_out[1, pl.ds(r, 1), :] = gas_a
            put(1, r, v_rows[1 + r] * keep + gas_r * couple)
            put(2, r, a_rows[r] * keep + gas_a * couple)

    def halo_in():
        @pl.when(has_prev)
        def _():
            to_next.wait_recv()
            q_rows[0:2] = edge_recv[0, 0:2].astype(F32)
            v_rows[0] = edge_recv[0, 2].astype(F32)

        @pl.when(t == 0)
        def _():
            q_rows[0:2] = jnp.zeros_like(q_rows[0:2])
            v_rows[0] = jnp.zeros_like(v_rows[0])

        @pl.when(has_next)
        def _():
            to_prev.wait_recv()
            q_rows[ROWS + 2 : ROWS + 4] = edge_recv[1, 0:2].astype(F32)
            v_rows[ROWS + 1] = edge_recv[1, 2].astype(F32)

        @pl.when(t == tiles - 1)
        def _():
            q_rows[ROWS + 2 : ROWS + 4] = jnp.zeros_like(q_rows[0:2])
            v_rows[ROWS + 1] = jnp.zeros_like(v_rows[0])

    def start(copies):
        for copy in copies:
            copy.start()

    def receive(copies):
        for copy in copies:
            copy.wait_recv()

    coef_from_mate.start()
    unpack(2, a_rows, 0)
    advect(0)
    launch(0)
    advect(1)
    launch(1)
    coef_from_mate.wait_recv()
    start(coef_y)
    halo_in()
    advect(2)
    launch(2)
    advect(3)
    launch(3)
    start(spread)
    take_mates(0)
    receive(coef_y)
    start(coef_x)
    take_mates(1)
    mate_relay(0, 1)
    sum_across()
    mate_relay(1, 1)
    take_mates(2)
    mate_relay(0, 2)
    take_mates(3)
    mate_relay(1, 2)
    mate_relay(2, 1)
    receive(coef_x)
    start(coef_core)
    mate_relay(3, 1)
    gas_step()
    load_coef.wait()
    own_receive(0)
    mate_relay(0, 3)
    mate_relay(2, 2)
    own_gains(0)
    mate_relay(3, 2)
    receive(coef_core)
    mate_gains(0)
    own_receive(1)
    mate_relay(1, 3)
    mate_gains(1)
    own_receive(2)
    mate_relay(2, 3)
    mate_gains(2)
    own_receive(3)
    mate_relay(3, 3)
    mate_gains(3)
    own_gains(1)
    own_gains(2)
    dust_speeds()
    own_gains(3)
    for c in range(CHUNKS):
        finish(c)

    @pl.when(has_next)
    def _():
        to_next.wait_send()

    @pl.when(has_prev)
    def _():
        to_prev.wait_send()

    for copy in [coef_from_mate, across] + coef_y + coef_x + coef_core + spread + shared:
        copy.wait_send()
    for c in range(CHUNKS):
        give(c).wait_send()
        for copy in own_items(c):
            copy.wait_send()
        gain_copy(c).wait_send()
    for place in range(QUAD):
        for up in (True, False):

            @pl.when((can_up if up else can_down) & (place <= w if up else place >= w))
            def _():
                pltpu.make_async_remote_copy(
                    src_ref=all_bins.at[:, pl.ds(0, 1)],
                    dst_ref=all_bins.at[:, pl.ds(0, 1)],
                    send_sem=(up_send if up else down_send).at[place],
                    recv_sem=item_recv.at[0, 0],
                    device_id=(t, mate),
                    device_id_type=MESH,
                ).wait_send()


def write_out(tiles, gas, rho_out, vr_out, va_out, gas_vr_out, gas_va_out, sem, gas_sem):
    copies = [pltpu.make_async_copy(gas.at[i], out, gas_sem.at[i]) for i, out in enumerate((gas_vr_out, gas_va_out))]
    for i, out in enumerate((rho_out, vr_out, va_out)):
        for l in range(tiles.shape[1]):
            lanes = pl.ds(l * LANES, LANES)
            copies.append(pltpu.make_async_copy(tiles.at[i, l], out.at[:, lanes], sem.at[i, l]))
    for copy in copies:
        copy.start()
    for copy in copies:
        copy.wait()


def step(split, tiles, rho, vr, va, gas_rho, gas_vr, gas_va, stop, coef):
    bins, rows, cells = rho.shape
    half = cells // 2
    flat = (bins * rows, cells)
    total_bins = coef.shape[1]
    xs, _, ys, cores = split
    coef = coef.reshape(bins * total_bins, total_bins)
    dma = pltpu.SemaphoreType.DMA
    hbm = pl.BlockSpec(memory_space=pltpu.HBM)
    vmem = pl.BlockSpec(memory_space=pltpu.VMEM)
    lane_tiles = cells // LANES
    out_shape = [jax.ShapeDtypeStruct(flat, F32)] * 3 + [jax.ShapeDtypeStruct((rows, cells), F32)] * 2
    results = pl.pallas_call(
        functools.partial(kernel, split, tiles),
        out_shape=[
            jax.ShapeDtypeStruct((3, lane_tiles, flat[0], LANES), F32),
            jax.ShapeDtypeStruct((2, rows, cells), F32),
        ],
        in_specs=[hbm] * 8,
        out_specs=[vmem] * 2,
        scratch_shapes=[
            pltpu.VMEM((3, lane_tiles, flat[0], LANES), F32),
            pltpu.VMEM((3, rows, cells), F32),
            pltpu.SMEM((bins,), F32),
            pltpu.VMEM(coef.shape, BF16),
            pltpu.VMEM((cores, xs, ys, coef.shape[0] // (cores * xs * ys), total_bins), BF16),
            pltpu.VMEM((rows + 4, bins, cells), F32),
            pltpu.VMEM((rows + 2, bins, cells), F32),
            pltpu.VMEM((rows, bins, cells), F32),
            pltpu.VMEM((2, 3, bins, cells), BF16),
            pltpu.VMEM((2, 3, bins, cells), BF16),
            pltpu.VMEM((rows, bins, cells), F32),
            pltpu.VMEM((CHUNKS, 2, DEEP, bins, half), BF16),
            pltpu.VMEM((CHUNKS, 2 * QUAD, DEEP, bins, half), BF16),
            pltpu.VMEM((QUAD, 8, cells), F32),
            pltpu.VMEM((QUAD, 8, cells), F32),
            pltpu.VMEM((2, 8, cells), F32),
            pltpu.VMEM((QUAD, 4, cells), F32),
            pltpu.VMEM((CHUNKS, DEEP, bins, half), BF16),
            pltpu.VMEM((CHUNKS, DEEP, bins, half), BF16),
            dma((5, lane_tiles)),
            dma((2,)),
            dma((2,)),
            dma((CHUNKS,)),
            dma((CHUNKS, 2 * QUAD)),
            dma((CHUNKS, QUAD)),
            dma((QUAD,)),
            dma((QUAD,)),
            dma((CHUNKS,)),
            dma((CHUNKS,)),
            dma((8,)),
            dma((8,)),
            dma((2 * QUAD,)),
            dma((2 * QUAD,)),
        ],
        compiler_params=pltpu.CompilerParams(
            collective_id=0, has_side_effects=True, vmem_limit_bytes=VMEM_BYTES
        ),
    )(
        *(
            pltpu.with_memory_space_constraint(x, pltpu.HBM)
            for x in (rho.reshape(flat), vr.reshape(flat), va.reshape(flat), coef, stop, gas_rho, gas_vr, gas_va)
        )
    )
    outs = pl.pallas_call(
        write_out,
        out_shape=out_shape,
        in_specs=[vmem] * 2,
        out_specs=[hbm] * 5,
        scratch_shapes=[dma((3, lane_tiles)), dma((2,))],
        compiler_params=pltpu.CompilerParams(vmem_limit_bytes=VMEM_BYTES),
    )(*results)
    return tuple(out.reshape(rho.shape) for out in outs[:3]) + tuple(outs[3:])


def solution(mesh):
    tiles = mesh.shape["tile"]
    grid = P("bin", "tile", None)
    gas = P("tile", None)
    return jax.shard_map(
        functools.partial(step, TILE_SPLIT[tiles], tiles),
        mesh=mesh,
        in_specs=(grid, grid, grid, gas, gas, gas, P("bin"), P("bin", None, None)),
        out_specs=(grid, grid, grid, gas, gas),
        check_vma=False,
    )
```
